32 devices in a mesh: drive: 2 (over y), tm: 4 (over z), mom: 2 (over x), col: 2 (over core).
Axes of the slice: x: 2, y: 2, z: 4, core: 2. Of those that a mesh axis runs over, the one named last changes fastest.
Arguments:
- propagators: float32 [8, 8, 384, 384], P(('drive', 'mom'), 'tm', None, 'col'), parts along dimension 0, as said below
- current_op: float32 [4, 384, 384], P('mom'), may hold values from -6 to 6
Outputs:
- spectrum: float32 [8, 2, 8, 384, 384], P(('drive', 'mom'), None, None, 'tm', 'col'), parts along dimension 0
The draws below stay inside these ranges and needn't reach their ends.
There are 2 independent parts, one for each index of `drive`. The reference program is written for one: setup_inputs(seed, part) draws one part's arguments, and reference() takes and returns one part's arrays. A program takes and returns all parts, laid end to end along the dimension named above; an argument that names none is the same for every part. Nothing has to cross between parts.
Inputs may be any that keep to these rules, and one draw needn't show every extreme that they name: Every matrix propagators[k, t] is orthogonal to float32 rounding, with dense entries.
All inputs are finite; a program needn't handle non-finite values.
Results may differ from the reference program's by a relative error of at most 0.0003.
Values sent between devices are 32-bit elements; how exact they have to be, the bound alone decides.
A program may use at most 64 MiB of HBM per device.

```python
import math
import jax
import jax.numpy as jnp
from jax import lax

K = 4
M = 384
TIME = 8


def draw_propagators(key, part):
    base = jax.random.normal(jax.random.fold_in(key, 7), (K, TIME, M, M), jnp.float32)
    ortho, upper = jnp.linalg.qr(base)
    diag = jnp.diagonal(upper, axis1=2, axis2=3)
    signs = jnp.where(diag >= 0, 1.0, -1.0).astype(jnp.float32)
    return (ortho * signs[:, :, None, :]).astype(jnp.float32)


def block_scale(stream_key, dims, shards, smallest, largest):
    def one(position, parts):
        draws = jax.random.uniform(jax.random.fold_in(jax.random.fold_in(stream_key, 6), position), (parts,), jnp.float32, smallest / len(shards), largest / len(shards))
        return jnp.repeat(jnp.exp(draws), dims[position] // parts).reshape((-1,) + (1,) * (len(dims) - position - 1))

    factor_of = one(*shards[0])
    for cut in shards[1:]:
        factor_of = factor_of * one(*cut)
    return factor_of


def centred(key, dims, scale, bound, shards=(), kind=jnp.bfloat16):
    array = jax.random.normal(key, dims, jnp.float32) * scale
    if len(shards) > 0:
        array = block_scale(key, dims, shards, -0.22, 0.18) * array
    return jnp.clip(array, min=-bound, max=bound).astype(kind)


def setup_inputs(seed: int = 0, part: int = 0) -> dict:
    key_of = jax.random.split(jax.random.key(seed), 3)
    part_splits = jax.random.split(jax.random.fold_in(key_of[2], part), 3)
    return {
        "propagators": draw_propagators(jax.random.fold_in(jax.random.fold_in(key_of[2], part), 71), part),
        "current_op": centred(key_of[1], (K, M, M), 1.0, 6.0, ((0, 2),), jnp.float32),
    }


def one_momentum(args):
    units, operator = args
    sym = 0.5 * (operator + operator.T)

    def advance(prefix, unit):
        prefix = jnp.dot(unit, prefix, precision=lax.Precision.HIGHEST)
        weighted = jnp.dot(sym, prefix, precision=lax.Precision.HIGHEST)
        heis = jnp.dot(prefix.T, weighted, precision=lax.Precision.HIGHEST)
        return (prefix, heis)
    start = jnp.eye(M, dtype=jnp.float32)
    _, history = lax.scan(advance, start, units)
    transformed = jnp.fft.fft(history, axis=0) / math.sqrt(TIME)
    return jnp.stack([jnp.real(transformed), jnp.imag(transformed)]).astype(jnp.float32)

def reference(propagators, current_op):
    return lax.map(one_momentum, (propagators, current_op))
```

```python
import functools
import math

import jax
import jax.numpy as jnp
from jax import lax
from jax.experimental import pallas as pl
from jax.experimental.pallas import tpu as pltpu
from jax.sharding import PartitionSpec as P

MESH = pl.DeviceIdType.MESH
NT = (((1,), (1,)), ((), ()))
NN = (((1,), (0,)), ((), ()))


def split(value):
    high = value.astype(jnp.bfloat16)
    low = (value - high.astype(jnp.float32)).astype(jnp.bfloat16)
    return high, low


def dot3(left, right, dims):
    def one(a, b):
        return lax.dot_general(a, b, dims, preferred_element_type=jnp.float32)

    rows = left[0].shape[0]
    both = one(jnp.concatenate(left, axis=0), right[0])
    return both[:rows] + (both[rows:] + one(left[0], right[1]))


def heis_kernel(nz, nc, chunks, u_ref, j_ref, out_ref, jbuf, ubuf, uhi, ulo, whi, wlo, shi, slo, total, pt, down, up, first, got,
                u_send, u_recv, u_local, j_local, i_send, i_recv, c_send, c_recv, x_send, x_recv, h_send, h_recv, f_send, f_recv):
    z = lax.axis_index("tm")
    c = lax.axis_index("col")
    kdev, slices, cw, order = u_ref.shape
    rw = order // nz
    ch = cw // chunks

    barrier = pltpu.get_barrier_semaphore()
    for dz in range(1, nz):
        pl.semaphore_signal(barrier, inc=1, device_id={"tm": lax.rem(z + dz, nz)}, device_id_type=MESH)
    for dc in range(1, nc):
        pl.semaphore_signal(barrier, inc=1, device_id={"col": lax.rem(c + dc, nc)}, device_id_type=MESH)
    own_half = pl.ds(pl.multiple_of(c * cw, 8), cw)
    own_block = pl.ds(pl.multiple_of(z * rw, 8), rw)
    local = []
    for k in range(kdev):
        copy = pltpu.make_async_copy(u_ref.at[k], ubuf.at[k, :, own_half], u_local.at[k])
        copy.start()
        local.append(copy)
    j_copy = pltpu.make_async_copy(j_ref, jbuf, j_local)
    j_copy.start()
    pl.semaphore_wait(barrier, nz + nc - 2)

    def u_copy(k, dc, half):
        return pltpu.make_async_remote_copy(
            u_ref.at[k], ubuf.at[k, :, pl.ds(pl.multiple_of(half * cw, 8), cw)],
            u_send.at[k, dc - 1], u_recv.at[k, dc - 1],
            device_id={"col": lax.rem(c + dc, nc)}, device_id_type=MESH)

    for k in range(kdev):
        for dc in range(1, nc):
            u_copy(k, dc, c).start()

    def part_rows(half, i):
        return pl.ds(pl.multiple_of(half * cw + i * ch, 8), ch)

    def carry_copy(k, i):
        rows = part_rows(c, i)
        return pltpu.make_async_remote_copy(
            pt.at[k, 1, rows], pt.at[k, 0, rows], c_send.at[k, i], c_recv.at[k, i],
            device_id={"tm": lax.rem(z + 1, nz)}, device_id_type=MESH)

    def core_copy(k, i, dc, half):
        rows = part_rows(half, i)
        return pltpu.make_async_remote_copy(
            pt.at[k, pl.ds(0, 2), rows], pt.at[k, pl.ds(0, 2), rows], x_send.at[k, i, dc - 1], x_recv.at[k, i, dc - 1],
            device_id={"col": lax.rem(c + dc, nc)}, device_id_type=MESH)

    def inner_copy(k, dc, half):
        rows = pl.ds(pl.multiple_of(half * cw, 8), cw)
        inner = pl.ds(2, slices - 1)
        return pltpu.make_async_remote_copy(
            pt.at[k, inner, rows], pt.at[k, inner, rows], i_send.at[k, dc - 1], i_recv.at[k, dc - 1],
            device_id={"col": lax.rem(c + dc, nc)}, device_id_type=MESH)

    def block_copy(source, k, peer, mine, slot):
        rows = pl.ds(pl.multiple_of(peer * rw, 8), rw)
        return pltpu.make_async_remote_copy(
            source.at[k, rows], out_ref.at[mine, k], h_send.at[k, slot], h_recv.at[k, slot],
            device_id={"tm": peer}, device_id_type=MESH)

    def first_copy(peer, slot):
        rows = pl.ds(pl.multiple_of(peer * rw, 8), rw)
        return pltpu.make_async_remote_copy(
            first.at[rows], got, f_send.at[slot], f_recv.at[0],
            device_id={"tm": peer}, device_id_type=MESH)

    def send_down(k):
        for d in range(nz - 1, 0, -1):
            @pl.when(z - d >= 0)
            def _():
                block_copy(down, k, lax.rem(z + nz - d, nz), z, d - 1).start()

    def send_up(k):
        for d in range(1, nz):
            @pl.when((z > 0) & (z + d < nz))
            def _():
                block_copy(up, k, lax.rem(z + d, nz), z, nz + d - 1).start()

    for k in range(kdev):
        local[k].wait()
        for dc in range(1, nc):
            u_copy(k, dc, lax.rem(c + nc - dc, nc)).wait_recv()
        product = ubuf[k, 0]
        for s in range(slices):
            uhi[k, s], ulo[k, s] = split(ubuf[k, s])
            if s:
                product = dot3(split(product), (uhi[k, s], ulo[k, s]), NN)
        whi[k], wlo[k] = split(product)

        @pl.when(z == 0)
        def _():
            total[...] = product
            row = lax.broadcasted_iota(jnp.int32, (cw, order), 0) + c * cw
            column = lax.broadcasted_iota(jnp.int32, (cw, order), 1)
            pt[k, 0, own_half] = jnp.where(row == column, 1.0, 0.0).astype(jnp.float32)
            pt[k, 1, own_half] = total[own_half]
            for i in range(chunks):
                carry_copy(k, i).start()

    j_copy.wait()
    for k in range(kdev):
        op = jbuf[k]
        shi[k], slo[k] = split(0.5 * (op + op.T))

    for k in range(kdev):
        for i in range(chunks):
            rows = part_rows(c, i)

            @pl.when(z > 0)
            def _():
                carry_copy(k, i).wait_recv()
                pt[k, 1, rows] = dot3(split(pt[k, 0, rows]), (whi[k], wlo[k]), NN)

            @pl.when((z > 0) & (z < nz - 1))
            def _():
                carry_copy(k, i).start()

            for dc in range(1, nc):
                core_copy(k, i, dc, c).start()
        if slices > 1:
            value = pt[k, 0, own_half]
            for s in range(slices - 1):
                value = dot3(split(value), (uhi[k, s], ulo[k, s]), NN)
                pt[k, 2 + s, own_half] = value
            for dc in range(1, nc):
                inner_copy(k, dc, c).start()
        if k > 0:
            send_up(k - 1)
        lines = jnp.concatenate([pt[k, s, own_half] for s in range(slices + 1)], axis=0)
        weighted = dot3(split(lines), (shi[k], slo[k]), NN)
        for i in range(chunks):
            for dc in range(1, nc):
                core_copy(k, i, dc, lax.rem(c + nc - dc, nc)).wait_recv()
        if slices > 1:
            for dc in range(1, nc):
                inner_copy(k, dc, lax.rem(c + nc - dc, nc)).wait_recv()
        parts = []
        for s in range(slices, -1, -1):
            at = s and (1 if s == slices else s + 1)
            right = split(weighted[at * cw:(at + 1) * cw])
            parts.insert(0, dot3(split(pt[k, at]), right, NT))
            if s == 1:
                down[k] = jnp.concatenate(parts, axis=1)
                send_down(k)
        up[k] = jnp.concatenate(parts[:-1], axis=1)
        for s in range(1, slices):
            at = (k * (slices - 1) + s - 1) * cw
            first[:, at:at + cw] = parts[s]
        out_ref[z, k] = down[k, own_block]

    send_up(kdev - 1)
    for d in range(1, nz):
        @pl.when(z == 0)
        def _():
            first_copy(lax.rem(z + d, nz), d - 1).start()

    for k in range(kdev):
        for d in range(1, nz):
            @pl.when(z + d < nz)
            def _():
                block_copy(down, k, lax.rem(z + d, nz), lax.rem(z + d, nz), d - 1).wait_recv()

            @pl.when(z - d > 0)
            def _():
                block_copy(up, k, lax.rem(z + nz - d, nz), lax.rem(z + nz - d, nz), nz + d - 1).wait_recv()

    @pl.when(z > 0)
    def _():
        first_copy(lax.rem(z, nz), 0).wait_recv()
        for k in range(kdev):
            for s in range(slices):
                if s == 0:
                    block = up[k, own_block][:, :cw]
                else:
                    at = (k * (slices - 1) + s - 1) * cw
                    block = got[:, at:at + cw]
                out_ref[0, k, :, s * cw:(s + 1) * cw] = block

    for k in range(kdev):
        for d in range(1, nz):
            @pl.when(z - d >= 0)
            def _():
                block_copy(down, k, lax.rem(z + nz - d, nz), z, d - 1).wait_send()

            @pl.when((z > 0) & (z + d < nz))
            def _():
                block_copy(up, k, lax.rem(z + d, nz), z, nz + d - 1).wait_send()
        for dc in range(1, nc):
            u_copy(k, dc, c).wait_send()
            if slices > 1:
                inner_copy(k, dc, c).wait_send()
        for i in range(chunks):
            for dc in range(1, nc):
                core_copy(k, i, dc, c).wait_send()

            @pl.when(z < nz - 1)
            def _():
                carry_copy(k, i).wait_send()
    for d in range(1, nz):
        @pl.when(z == 0)
        def _():
            first_copy(lax.rem(z + d, nz), d - 1).wait_send()


def real_dft(values):
    length = len(values)
    if length == 1:
        return [(values[0], None)]
    if length % 2:
        found = []
        for f in range(length):
            re = sum(math.cos(2 * math.pi * f * t / length) * v for t, v in enumerate(values))
            im = sum(-math.sin(2 * math.pi * f * t / length) * v for t, v in enumerate(values))
            found.append((re, im if f else None))
        return found
    half = length // 2
    even, odd = real_dft(values[0::2]), real_dft(values[1::2])
    found = [None] * length
    for f in range(half // 2 + 1):
        (er, ei), (dr, di) = even[f % half], odd[f % half]
        angle = -2 * math.pi * f / length
        if f == 0:
            tr, ti = dr, di
        elif 4 * f == length:
            tr, ti = di, -dr
        else:
            wr, wi = math.cos(angle), math.sin(angle)
            tr = wr * dr if di is None else wr * dr - wi * di
            ti = wi * dr if di is None else wr * di + wi * dr

        def add(a, b, sign):
            if b is None:
                return a
            if a is None:
                return b if sign > 0 else -b
            return a + b if sign > 0 else a - b

        found[f] = (add(er, tr, 1), add(ei, ti, 1))
        found[f + half] = (add(er, tr, -1), add(ei, ti, -1))
    for f in range(length):
        if found[f] is None:
            re, im = found[length - f]
            found[f] = (re, None if im is None else -im)
    return found


def dft_kernel(h_ref, out_ref):
    nz, rows, width = h_ref.shape[0], h_ref.shape[2], h_ref.shape[3]
    length, cw = out_ref.shape[2], out_ref.shape[4]
    scale = 1.0 / math.sqrt(length)
    slices = width // cw
    mine = lax.axis_index("tm") * slices

    def at(slot, s):
        return h_ref[slot, 0, :, s * cw:(s + 1) * cw]

    values = []
    for t in range(nz * slices):
        value = at(t // slices, t % slices)
        if t + 1 < nz * slices:
            value = jnp.where(t < mine, at((t + 1) // slices, (t + 1) % slices), value)
            value = jnp.where(t + 1 == mine, at(0, 0), value)
        values.append(value * scale)
    for f, (re, im) in enumerate(real_dft(values)):
        out_ref[0, 0, f] = re
        out_ref[0, 1, f] = jnp.zeros((rows, cw), jnp.float32) if im is None else im


def body(nz, nc, propagators, current_op):
    turned = jnp.swapaxes(propagators, 2, 3)
    kdev, slices, cw, order = turned.shape
    rw = order // nz
    chunks = 4
    first = max(128, -(-kdev * (slices - 1) * cw // 128) * 128)
    dma = pltpu.SemaphoreType.DMA
    blocks = pl.pallas_call(
        functools.partial(heis_kernel, nz, nc, chunks),
        out_shape=jax.ShapeDtypeStruct((nz, kdev, rw, slices * cw), jnp.float32),
        in_specs=[pl.BlockSpec(memory_space=pl.ANY), pl.BlockSpec(memory_space=pl.ANY)],
        out_specs=pl.BlockSpec(memory_space=pltpu.VMEM),
        scratch_shapes=[
            pltpu.VMEM((kdev, order, order), jnp.float32),
            pltpu.VMEM((kdev, slices, order, order), jnp.float32),
            pltpu.VMEM((kdev, slices, order, order), jnp.bfloat16),
            pltpu.VMEM((kdev, slices, order, order), jnp.bfloat16),
            pltpu.VMEM((kdev, order, order), jnp.bfloat16),
            pltpu.VMEM((kdev, order, order), jnp.bfloat16),
            pltpu.VMEM((kdev, order, order), jnp.bfloat16),
            pltpu.VMEM((kdev, order, order), jnp.bfloat16),
            pltpu.VMEM((order, order), jnp.float32),
            pltpu.VMEM((kdev, slices + 1, order, order), jnp.float32),
            pltpu.VMEM((kdev, order, slices * cw), jnp.float32),
            pltpu.VMEM((kdev, order, slices * cw), jnp.float32),
            pltpu.VMEM((order, first), jnp.float32),
            pltpu.VMEM((rw, first), jnp.float32),
            dma((kdev, nc)), dma((kdev, nc)), dma((kdev,)), dma, dma((kdev, nc)), dma((kdev, nc)),
            dma((kdev, chunks)), dma((kdev, chunks)),
            dma((kdev, chunks, nc)), dma((kdev, chunks, nc)),
            dma((kdev, 2 * nz)), dma((kdev, 2 * nz)), dma((nz,)), dma((1,)),
        ],
        compiler_params=pltpu.CompilerParams(
            collective_id=0, has_side_effects=True, vmem_limit_bytes=60 * 2**20),
    )(turned, current_op)
    length = nz * slices
    step = rw // 2 if rw % 16 == 0 else rw
    return pl.pallas_call(
        dft_kernel,
        grid=(kdev, rw // step),
        out_shape=jax.ShapeDtypeStruct((kdev, 2, length, rw, cw), jnp.float32),
        in_specs=[pl.BlockSpec((nz, 1, step, slices * cw), lambda k, r: (0, k, r, 0))],
        out_specs=pl.BlockSpec((1, 2, length, step, cw), lambda k, r: (k, 0, 0, r, 0)),
        compiler_params=pltpu.CompilerParams(vmem_limit_bytes=32 * 2**20),
    )(blocks)


def solution(mesh):
    return jax.shard_map(
        functools.partial(body, mesh.shape["tm"], mesh.shape["col"]),
        mesh=mesh,
        in_specs=(P(("drive", "mom"), "tm", None, "col"), P("mom", None, None)),
        out_specs=P(("drive", "mom"), None, None, "tm", "col"),
        check_vma=False,
    )
```

```python
import functools
import math

import jax
import jax.numpy as jnp
from jax import lax
from jax.experimental import pallas as pl
from jax.experimental.pallas import tpu as pltpu
from jax.sharding import PartitionSpec as P

MESH = pl.DeviceIdType.MESH
NT = (((1,), (1,)), ((), ()))
NN = (((1,), (0,)), ((), ()))


def split(value):
    high = value.astype(jnp.bfloat16)
    low = (value - high.astype(jnp.float32)).astype(jnp.bfloat16)
    return high, low


def dot3(left, right, dims):
    def one(a, b):
        return lax.dot_general(a, b, dims, preferred_element_type=jnp.float32)

    rows = left[0].shape[0]
    both = one(jnp.concatenate(left, axis=0), right[0])
    return both[:rows] + (both[rows:] + one(left[0], right[1]))


def heis_kernel(nz, nc, chunks, u_ref, j_ref, out_ref, jbuf, ubuf, uhi, ulo, whi, wlo, shi, slo, total, pt, down, up, first, got,
                u_send, u_recv, u_local, j_local, i_send, i_recv, c_send, c_recv, x_send, x_recv, h_send, h_recv, f_send, f_recv):
    z = lax.axis_index("tm")
    c = lax.axis_index("col")
    kdev, slices, cw, order = u_ref.shape
    rw = order // nz
    ch = cw // chunks

    barrier = pltpu.get_barrier_semaphore()
    for dz in range(1, nz):
        pl.semaphore_signal(barrier, inc=1, device_id={"tm": lax.rem(z + dz, nz)}, device_id_type=MESH)
    for dc in range(1, nc):
        pl.semaphore_signal(barrier, inc=1, device_id={"col": lax.rem(c + dc, nc)}, device_id_type=MESH)
    own_half = pl.ds(pl.multiple_of(c * cw, 8), cw)
    own_block = pl.ds(pl.multiple_of(z * rw, 8), rw)
    local = []
    for k in range(kdev):
        copy = pltpu.make_async_copy(u_ref.at[k], ubuf.at[k, :, own_half], u_local.at[k])
        copy.start()
        local.append(copy)
    j_copy = pltpu.make_async_copy(j_ref, jbuf, j_local)
    j_copy.start()
    pl.semaphore_wait(barrier, nz + nc - 2)

    def u_copy(k, dc, half):
        return pltpu.make_async_remote_copy(
            u_ref.at[k], ubuf.at[k, :, pl.ds(pl.multiple_of(half * cw, 8), cw)],
            u_send.at[k, dc - 1], u_recv.at[k, dc - 1],
            device_id={"col": lax.rem(c + dc, nc)}, device_id_type=MESH)

    for k in range(kdev):
        for dc in range(1, nc):
            u_copy(k, dc, c).start()

    def part_rows(half, i):
        return pl.ds(pl.multiple_of(half * cw + i * ch, 8), ch)

    def carry_copy(k, i):
        rows = part_rows(c, i)
        return pltpu.make_async_remote_copy(
            pt.at[k, 1, rows], pt.at[k, 0, rows], c_send.at[k, i], c_recv.at[k, i],
            device_id={"tm": lax.rem(z + 1, nz)}, device_id_type=MESH)

    def core_copy(k, i, dc, half):
        rows = part_rows(half, i)
        return pltpu.make_async_remote_copy(
            pt.at[k, pl.ds(0, 2), rows], pt.at[k, pl.ds(0, 2), rows], x_send.at[k, i, dc - 1], x_recv.at[k, i, dc - 1],
            device_id={"col": lax.rem(c + dc, nc)}, device_id_type=MESH)

    def inner_copy(k, dc, half):
        rows = pl.ds(pl.multiple_of(half * cw, 8), cw)
        inner = pl.ds(2, slices - 1)
        return pltpu.make_async_remote_copy(
            pt.at[k, inner, rows], pt.at[k, inner, rows], i_send.at[k, dc - 1], i_recv.at[k, dc - 1],
            device_id={"col": lax.rem(c + dc, nc)}, device_id_type=MESH)

    def block_copy(source, k, peer, mine, slot):
        rows = pl.ds(pl.multiple_of(peer * rw, 8), rw)
        return pltpu.make_async_remote_copy(
            source.at[k, rows], out_ref.at[mine, k], h_send.at[k, slot], h_recv.at[k, slot],
            device_id={"tm": peer}, device_id_type=MESH)

    def first_copy(peer, slot):
        rows = pl.ds(pl.multiple_of(peer * rw, 8), rw)
        return pltpu.make_async_remote_copy(
            first.at[rows], got, f_send.at[slot], f_recv.at[0],
            device_id={"tm": peer}, device_id_type=MESH)

    def send_down(k):
        for d in range(nz - 1, 0, -1):
            @pl.when(z - d >= 0)
            def _():
                block_copy(down, k, lax.rem(z + nz - d, nz), z, d - 1).start()

    def send_up(k):
        for d in range(1, nz):
            @pl.when((z > 0) & (z + d < nz))
            def _():
                block_copy(up, k, lax.rem(z + d, nz), z, nz + d - 1).start()

    for k in range(kdev):
        local[k].wait()
        for dc in range(1, nc):
            u_copy(k, dc, lax.rem(c + nc - dc, nc)).wait_recv()
        product = ubuf[k, 0]
        for s in range(slices):
            uhi[k, s], ulo[k, s] = split(ubuf[k, s])
            if s:
                product = dot3(split(product), (uhi[k, s], ulo[k, s]), NN)
        whi[k], wlo[k] = split(product)

        @pl.when(z == 0)
        def _():
            total[...] = product
            row = lax.broadcasted_iota(jnp.int32, (cw, order), 0) + c * cw
            column = lax.broadcasted_iota(jnp.int32, (cw, order), 1)
            pt[k, 0, own_half] = jnp.where(row == column, 1.0, 0.0).astype(jnp.float32)
            pt[k, 1, own_half] = total[own_half]
            for i in range(chunks):
                carry_copy(k, i).start()

    j_copy.wait()
    for k in range(kdev):
        op = jbuf[k]
        shi[k], slo[k] = split(0.5 * (op + op.T))

    for k in range(kdev):
        for i in range(chunks):
            rows = part_rows(c, i)

            @pl.when(z > 0)
            def _():
                carry_copy(k, i).wait_recv()
                pt[k, 1, rows] = dot3(split(pt[k, 0, rows]), (whi[k], wlo[k]), NN)

            @pl.when((z > 0) & (z < nz - 1))
            def _():
                carry_copy(k, i).start()

            for dc in range(1, nc):
                core_copy(k, i, dc, c).start()
        if slices > 1:
            value = pt[k, 0, own_half]
            for s in range(slices - 1):
                value = dot3(split(value), (uhi[k, s], ulo[k, s]), NN)
                pt[k, 2 + s, own_half] = value
            for dc in range(1, nc):
                inner_copy(k, dc, c).start()
        if k > 0:
            send_up(k - 1)
        lines = jnp.concatenate([pt[k, s, own_half] for s in range(slices + 1)], axis=0)
        weighted = dot3(split(lines), (shi[k], slo[k]), NN)
        for i in range(chunks):
            for dc in range(1, nc):
                core_copy(k, i, dc, lax.rem(c + nc - dc, nc)).wait_recv()
        if slices > 1:
            for dc in range(1, nc):
                inner_copy(k, dc, lax.rem(c + nc - dc, nc)).wait_recv()
        parts = []
        for s in range(slices, -1, -1):
            at = s and (1 if s == slices else s + 1)
            right = split(weighted[at * cw:(at + 1) * cw])
            parts.insert(0, dot3(split(pt[k, at]), right, NT))
            if s == 1:
                down[k] = jnp.concatenate(parts, axis=1)
                send_down(k)
        up[k] = jnp.concatenate(parts[:-1], axis=1)
        for s in range(1, slices):
            at = (k * (slices - 1) + s - 1) * cw
            first[:, at:at + cw] = parts[s]
        out_ref[z, k] = down[k, own_block]

    send_up(kdev - 1)
    for d in range(1, nz):
        @pl.when(z == 0)
        def _():
            first_copy(lax.rem(z + d, nz), d - 1).start()

    for k in range(kdev):
        for d in range(1, nz):
            @pl.when(z + d < nz)
            def _():
                block_copy(down, k, lax.rem(z + d, nz), lax.rem(z + d, nz), d - 1).wait_recv()

            @pl.when(z - d > 0)
            def _():
                block_copy(up, k, lax.rem(z + nz - d, nz), lax.rem(z + nz - d, nz), nz + d - 1).wait_recv()

    @pl.when(z > 0)
    def _():
        first_copy(lax.rem(z, nz), 0).wait_recv()
        for k in range(kdev):
            for s in range(slices):
                if s == 0:
                    block = up[k, own_block][:, :cw]
                else:
                    at = (k * (slices - 1) + s - 1) * cw
                    block = got[:, at:at + cw]
                out_ref[0, k, :, s * cw:(s + 1) * cw] = block

    for k in range(kdev):
        for d in range(1, nz):
            @pl.when(z - d >= 0)
            def _():
                block_copy(down, k, lax.rem(z + nz - d, nz), z, d - 1).wait_send()

            @pl.when((z > 0) & (z + d < nz))
            def _():
                block_copy(up, k, lax.rem(z + d, nz), z, nz + d - 1).wait_send()
        for dc in range(1, nc):
            u_copy(k, dc, c).wait_send()
            if slices > 1:
                inner_copy(k, dc, c).wait_send()
        for i in range(chunks):
            for dc in range(1, nc):
                core_copy(k, i, dc, c).wait_send()

            @pl.when(z < nz - 1)
            def _():
                carry_copy(k, i).wait_send()
    for d in range(1, nz):
        @pl.when(z == 0)
        def _():
            first_copy(lax.rem(z + d, nz), d - 1).wait_send()


def real_dft(values):
    length = len(values)
    if length == 1:
        return [(values[0], None)]
    if length % 2:
        found = []
        for f in range(length):
            re = sum(math.cos(2 * math.pi * f * t / length) * v for t, v in enumerate(values))
            im = sum(-math.sin(2 * math.pi * f * t / length) * v for t, v in enumerate(values))
            found.append((re, im if f else None))
        return found
    half = length // 2
    even, odd = real_dft(values[0::2]), real_dft(values[1::2])
    found = [None] * length
    for f in range(half // 2 + 1):
        (er, ei), (dr, di) = even[f % half], odd[f % half]
        angle = -2 * math.pi * f / length
        if f == 0:
            tr, ti = dr, di
        elif 4 * f == length:
            tr, ti = di, -dr
        else:
            wr, wi = math.cos(angle), math.sin(angle)
            tr = wr * dr if di is None else wr * dr - wi * di
            ti = wi * dr if di is None else wr * di + wi * dr

        def add(a, b, sign):
            if b is None:
                return a
            if a is None:
                return b if sign > 0 else -b
            return a + b if sign > 0 else a - b

        found[f] = (add(er, tr, 1), add(ei, ti, 1))
        found[f + half] = (add(er, tr, -1), add(ei, ti, -1))
    for f in range(length):
        if found[f] is None:
            re, im = found[length - f]
            found[f] = (re, None if im is None else -im)
    return found


def dft_kernel(h_ref, out_ref):
    nz, rows, width = h_ref.shape[0], h_ref.shape[2], h_ref.shape[3]
    length, cw = out_ref.shape[2], out_ref.shape[4]
    scale = 1.0 / math.sqrt(length)
    slices = width // cw
    mine = lax.axis_index("tm") * slices

    def at(slot, s):
        return h_ref[slot, 0, :, s * cw:(s + 1) * cw]

    values = []
    for t in range(nz * slices):
        value = at(t // slices, t % slices)
        if t + 1 < nz * slices:
            value = jnp.where(t < mine, at((t + 1) // slices, (t + 1) % slices), value)
            value = jnp.where(t + 1 == mine, at(0, 0), value)
        values.append(value * scale)
    for f, (re, im) in enumerate(real_dft(values)):
        out_ref[0, 0, f] = re
        out_ref[0, 1, f] = jnp.zeros((rows, cw), jnp.float32) if im is None else im


def body(nz, nc, propagators, current_op):
    turned = jnp.swapaxes(propagators, 2, 3)
    kdev, slices, cw, order = turned.shape
    rw = order // nz
    chunks = 6
    first = max(128, -(-kdev * (slices - 1) * cw // 128) * 128)
    dma = pltpu.SemaphoreType.DMA
    blocks = pl.pallas_call(
        functools.partial(heis_kernel, nz, nc, chunks),
        out_shape=jax.ShapeDtypeStruct((nz, kdev, rw, slices * cw), jnp.float32),
        in_specs=[pl.BlockSpec(memory_space=pl.ANY), pl.BlockSpec(memory_space=pl.ANY)],
        out_specs=pl.BlockSpec(memory_space=pltpu.VMEM),
        scratch_shapes=[
            pltpu.VMEM((kdev, order, order), jnp.float32),
            pltpu.VMEM((kdev, slices, order, order), jnp.float32),
            pltpu.VMEM((kdev, slices, order, order), jnp.bfloat16),
            pltpu.VMEM((kdev, slices, order, order), jnp.bfloat16),
            pltpu.VMEM((kdev, order, order), jnp.bfloat16),
            pltpu.VMEM((kdev, order, order), jnp.bfloat16),
            pltpu.VMEM((kdev, order, order), jnp.bfloat16),
            pltpu.VMEM((kdev, order, order), jnp.bfloat16),
            pltpu.VMEM((order, order), jnp.float32),
            pltpu.VMEM((kdev, slices + 1, order, order), jnp.float32),
            pltpu.VMEM((kdev, order, slices * cw), jnp.float32),
            pltpu.VMEM((kdev, order, slices * cw), jnp.float32),
            pltpu.VMEM((order, first), jnp.float32),
            pltpu.VMEM((rw, first), jnp.float32),
            dma((kdev, nc)), dma((kdev, nc)), dma((kdev,)), dma, dma((kdev, nc)), dma((kdev, nc)),
            dma((kdev, chunks)), dma((kdev, chunks)),
            dma((kdev, chunks, nc)), dma((kdev, chunks, nc)),
            dma((kdev, 2 * nz)), dma((kdev, 2 * nz)), dma((nz,)), dma((1,)),
        ],
        compiler_params=pltpu.CompilerParams(
            collective_id=0, has_side_effects=True, vmem_limit_bytes=60 * 2**20),
    )(turned, current_op)
    length = nz * slices
    step = rw // 2 if rw % 16 == 0 else rw
    return pl.pallas_call(
        dft_kernel,
        grid=(kdev, rw // step),
        out_shape=jax.ShapeDtypeStruct((kdev, 2, length, rw, cw), jnp.float32),
        in_specs=[pl.BlockSpec((nz, 1, step, slices * cw), lambda k, r: (0, k, r, 0))],
        out_specs=pl.BlockSpec((1, 2, length, step, cw), lambda k, r: (k, 0, 0, r, 0)),
        compiler_params=pltpu.CompilerParams(vmem_limit_bytes=32 * 2**20),
    )(blocks)


def solution(mesh):
    return jax.shard_map(
        functools.partial(body, mesh.shape["tm"], mesh.shape["col"]),
        mesh=mesh,
        in_specs=(P(("drive", "mom"), "tm", None, "col"), P("mom", None, None)),
        out_specs=P(("drive", "mom"), None, None, "tm", "col"),
        check_vma=False,
    )
```
